256 devices in a mesh: bin: 16 (over y, x_hi, core), coil: 16 (over z, x_lo).
Axes of the slice: x: 4 (x_hi: 2, x_lo: 2; x = x_hi * 2 + x_lo), y: 4, z: 8, core: 2. Of those that a mesh axis runs over, the one named last changes fastest.
Arguments:
- cine_image: bfloat16 [16, 256, 8, 256], P('bin', 'coil'), may hold values from -6 to 6
- warp_blocks: bfloat16 [16, 4096, 2, 4096], P('bin', 'coil'), may hold values from -0.5 to 0.5
- warp_index: int32 [16, 4096, 2], P('bin', 'coil'), may hold values from 0 to 4095, as said below
- sample_mask: int32 [16, 256, 128], P('bin'), may hold values 0 or 1
- kspace_data: bfloat16 [16, 32, 256, 8, 256], P('bin', 'coil'), may hold values from -6 to 6
- sensitivity: bfloat16 [32, 256, 8, 256], P(None, 'coil'), may hold values from -1.5 to 1.5
Outputs:
- gradient: float32 [16, 256, 8, 256], P('bin', 'coil')
The draws below stay inside these ranges and needn't reach their ends.
Inputs may be any that keep to these rules, and one draw needn't show every extreme that they name: `warp_index`: slot 0 of every block names the block itself; every other slot of the block at row y names a block whose row lies among the 16 rows from 16 * (y // 16) on.
All inputs are finite; a program needn't handle non-finite values. No bound on the sum of `sample_mask` on one device may be relied on, other than what follows from the above.
Results may differ from the reference program's by a relative error of at most 0.017.
Values may be sent and summed in bfloat16 or wider, within the bound.
No kernel may reach another device: no remote copies, remote signals or barrier semaphores. Data moves between devices by JAX's collectives and lax.ppermute only.
A program may use at most 128 MiB of HBM per device.

```python
import jax
import jax.numpy as jnp
from jax import lax

NY = 256
NX = 128
Z = 8
BLOCK = 64
K = 2
BAND = 16
BINS = 16
COILS = 32
NBLK = 4096


def draw_warp_index(key, part):
    strips = NX // BLOCK
    block_total = NY * Z * strips
    serial = jnp.arange(block_total, dtype=jnp.int32)
    row_number = serial // (Z * strips)
    band_start = row_number // BAND * BAND
    key_row, key_depth, key_strip = jax.random.split(key, 3)
    draw_shape = (BINS, block_total, K - 1)
    row_choice = band_start[None, :, None] + jax.random.randint(key_row, draw_shape, 0, BAND, dtype=jnp.int32)
    depth_choice = jax.random.randint(key_depth, draw_shape, 0, Z, dtype=jnp.int32)
    strip_choice = jax.random.randint(key_strip, draw_shape, 0, strips, dtype=jnp.int32)
    others = (row_choice * Z + depth_choice) * strips + strip_choice
    own_slot = jnp.broadcast_to(serial[None, :, None], (BINS, block_total, 1))
    return jnp.concatenate([own_slot, others], axis=2).astype(jnp.int32)


def place_ends(drawn, key, smallest, largest):
    longest = drawn.shape.index(max(drawn.shape))
    spots = []
    for shift in (0, 1):
        where = [jax.random.randint(jax.random.fold_in(key, axis), (), 0, length) for axis, length in enumerate(drawn.shape)]
        where[longest] = (where[longest] + shift) % drawn.shape[longest]
        spots.append(tuple(where))
    return drawn.at[spots[0]].set(smallest).at[spots[1]].set(largest)


def block_levels(key, extent, shards, smallest, high):
    level, own = 1.0, jax.random.fold_in(key, 6)
    for dim, blocks in shards:
        steps = jnp.exp(jax.random.uniform(jax.random.fold_in(own, dim), (blocks,), jnp.float32, smallest / len(shards), high / len(shards)))
        level = level * jnp.repeat(steps, extent[dim] // blocks).reshape([-1 if axis == dim else 1 for axis in range(len(extent))])
    return level


def noise(stream_key, dims, scale, bound, cuts=(), kind=jnp.bfloat16):
    values = scale * jax.random.normal(stream_key, dims, jnp.float32)
    if cuts:
        values = values * block_levels(stream_key, dims, cuts, -0.22, 0.18)
    return jnp.clip(values, -bound, bound).astype(kind)


def setup_inputs(seed: int = 0) -> dict:
    streams_of = jax.random.split(jax.random.key(seed), 7)
    return {
        "cine_image": noise(streams_of[0], (BINS, NY, Z, 2 * NX), 1.0, 6.0, ((0, 16), (1, 16))),
        "warp_blocks": noise(streams_of[1], (BINS, NBLK, K, BLOCK * BLOCK), (K * BLOCK) ** -0.5, 0.5, ((0, 16), (1, 16))),
        "warp_index": draw_warp_index(jax.random.fold_in(streams_of[6], 71), 0),
        "sample_mask": place_ends((jax.random.randint(streams_of[3], (BINS, NY, NX), 0, 3) < 1).astype(jnp.int32), jax.random.fold_in(streams_of[3], 1), 0, 1),
        "kspace_data": noise(streams_of[4], (BINS, COILS, NY, Z, 2 * NX), 1.0, 6.0, ((0, 16), (1, 16))),
        "sensitivity": noise(streams_of[5], (COILS, NY, Z, 2 * NX), 0.25, 1.5, ((1, 16),)),
    }


def cosine_sine(length):
    positions = jnp.arange(length, dtype=jnp.int32)
    phases = positions[:, None] * positions[None, :] % length
    angles = phases.astype(jnp.float32) * (2.0 * jnp.pi / length)
    factor = 1.0 / jnp.sqrt(jnp.asarray(length, jnp.float32))
    return (jnp.cos(angles) * factor, jnp.sin(angles) * factor)

def make_row_matrix(length):
    cosine_table, sine_table = cosine_sine(length)
    upper_half = jnp.concatenate([cosine_table, -sine_table], axis=1)
    lower_half = jnp.concatenate([sine_table, cosine_table], axis=1)
    return jnp.concatenate([upper_half, lower_half], axis=0).astype(jnp.bfloat16)

def make_column_tables(length):
    cosine_table, sine_table = cosine_sine(length)
    return jnp.stack([cosine_table, sine_table]).astype(jnp.bfloat16)

def row_apply(values, row_matrix, inverse):
    flattened = values.reshape(-1, values.shape[-1])
    table_used = row_matrix.T if inverse else row_matrix
    return jnp.dot(flattened, table_used, preferred_element_type=jnp.float32).reshape(values.shape)

def column_transform(values, tables, inverse):
    products = jnp.einsum('tky,cyzx->tckzx', tables.astype(jnp.float32), values.astype(jnp.float32))
    direct, turned = (products[0], products[1])
    half_width = direct.shape[-1] // 2
    if inverse:
        swapped = jnp.concatenate([-turned[..., half_width:], turned[..., :half_width]], axis=-1)
    else:
        swapped = jnp.concatenate([turned[..., half_width:], -turned[..., :half_width]], axis=-1)
    return direct + swapped

def coil_images(sensitivity, moved_image):
    half_width = moved_image.shape[-1] // 2
    sens_re = sensitivity[..., :half_width].astype(jnp.float32)
    sens_im = sensitivity[..., half_width:].astype(jnp.float32)
    image_re = moved_image[..., :half_width].astype(jnp.float32)
    image_im = moved_image[..., half_width:].astype(jnp.float32)
    real_part = sens_re * image_re - sens_im * image_im
    imag_part = sens_re * image_im + sens_im * image_re
    return jnp.concatenate([real_part, imag_part], axis=-1).astype(jnp.bfloat16)

def conj_sum(sensitivity, back_rows):
    half_width = back_rows.shape[-1] // 2
    sens_re = sensitivity[..., :half_width].astype(jnp.float32)
    sens_im = sensitivity[..., half_width:].astype(jnp.float32)
    back_re = back_rows[..., :half_width]
    back_im = back_rows[..., half_width:]
    real_part = lax.optimization_barrier(jnp.sum(sens_re * back_re + sens_im * back_im, axis=0))
    imag_part = lax.optimization_barrier(jnp.sum(sens_re * back_im - sens_im * back_re, axis=0))
    return jnp.concatenate([real_part, imag_part], axis=-1)

def split_blocks(values):
    row_count, depth_count, full_width = values.shape
    grouped = values.reshape(row_count, depth_count, 2, full_width // (2 * BLOCK), BLOCK)
    return grouped.transpose(0, 1, 3, 2, 4).reshape(-1, 2, BLOCK)

def join_blocks(pieces, row_count, depth_count, full_width):
    grouped = pieces.reshape(row_count, depth_count, full_width // (2 * BLOCK), 2, BLOCK)
    return grouped.transpose(0, 1, 3, 2, 4).reshape(row_count, depth_count, full_width)

def warp_forward(source, weights, block_index):
    pieces = split_blocks(source)
    chosen = jnp.take(pieces, block_index, axis=0)
    matrices = weights.reshape(weights.shape[0], weights.shape[1], BLOCK, BLOCK)
    return jnp.einsum('ikpq,ikcq->icp', matrices.astype(jnp.float32), chosen.astype(jnp.float32))

def warp_adjoint(values, weights, block_index):
    matrices = weights.reshape(weights.shape[0], weights.shape[1], BLOCK, BLOCK)
    contributions = jnp.einsum('ikpq,icp->ikcq', matrices.astype(jnp.float32), values.astype(jnp.float32))
    flattened = contributions.reshape(-1, 2, BLOCK)
    zeros_start = jnp.zeros((values.shape[0], 2, BLOCK), jnp.float32)
    return zeros_start.at[block_index.reshape(-1)].add(flattened)

def reference(cine_image, warp_blocks, warp_index, sample_mask, kspace_data, sensitivity):
    row_matrix = make_row_matrix(NX)
    column_tables = make_column_tables(NY)
    prior_frames = jnp.roll(cine_image, 1, axis=0)

    def forward_bin(operands):
        current, earlier, weights, block_index = operands
        warped = join_blocks(warp_forward(earlier, weights, block_index), NY, Z, 2 * NX)
        return (current.astype(jnp.float32) + warped).astype(jnp.bfloat16)
    moved_image = lax.map(forward_bin, (cine_image, prior_frames, warp_blocks, warp_index))

    def data_bin(operands):
        current, mask_now, measured = operands
        images = coil_images(sensitivity, current)
        row_spectra = row_apply(images, row_matrix, False).astype(jnp.bfloat16)
        spectra = column_transform(row_spectra, column_tables, False)
        weight_mask = jnp.concatenate([mask_now, mask_now], axis=1).astype(jnp.float32)[:, None, :]
        residual = (weight_mask * (spectra - measured.astype(jnp.float32))).astype(jnp.bfloat16)
        back_columns = column_transform(residual, column_tables, True).astype(jnp.bfloat16)
        back_rows = row_apply(back_columns, row_matrix, True)
        return conj_sum(sensitivity, back_rows)
    data_grad = lax.map(data_bin, (moved_image, sample_mask, kspace_data))

    def adjoint_bin(operands):
        grad_now, weights, block_index = operands
        pieces = split_blocks(grad_now.astype(jnp.bfloat16))
        summed = warp_adjoint(pieces, weights, block_index)
        return join_blocks(summed, NY, Z, 2 * NX).astype(jnp.bfloat16)
    pulled = lax.map(adjoint_bin, (data_grad, warp_blocks, warp_index))
    return data_grad + jnp.roll(pulled, -1, axis=0).astype(jnp.float32)
```

```python
import functools

import jax
import jax.numpy as jnp
import numpy as np
from jax import lax
from jax.experimental import pallas as pl
from jax.experimental.pallas import tpu as pltpu
from jax.sharding import Mesh
from jax.sharding import PartitionSpec as P

NY = 256
NX = 128
Z = 8
COILS = 32
SHARE = 4
STEP = 32
PAIR = 2

F32 = jnp.float32
BF16 = jnp.bfloat16


def cosine_sine(length):
    positions = np.arange(length)
    phases = positions[:, None] * positions[None, :] % length
    angles = phases * (2.0 * np.pi / length)
    return np.cos(angles) / np.sqrt(length), np.sin(angles) / np.sqrt(length)


def row_matrix():
    cosine, sine = cosine_sine(NX)
    return np.block([[cosine, -sine], [sine, cosine]]).astype(BF16)


def column_table():
    return np.concatenate(cosine_sine(NY), axis=1).astype(BF16)


def iota(shape, axis):
    return lax.broadcasted_iota(jnp.int32, shape, axis)


def matmul(a, b):
    return jnp.dot(a, b, preferred_element_type=F32)


def high_low(values):
    high = values.astype(BF16)
    return high, (values - high.astype(F32)).astype(BF16)


def sublane_roles(rows):
    r = iota((rows, 128), 0)
    return r, (r >> 2) & 1, (r >> 1) & 1, r & 1


def shift_lanes(values, distance):
    return jnp.where(
        distance == 1,
        pltpu.roll(values, 1, 1),
        jnp.where(distance == -1, pltpu.roll(values, 127, 1), values),
    )


def depth_major():
    to, frm = iota((128, 128), 0), iota((128, 128), 1)
    return ((to & 15) * Z + (to >> 4) == frm).astype(F32).astype(BF16)


def warp_kernel(share, col_ref, w_ref, prior_ref, cur_ref, out_ref, acc_ref):
    step = pl.program_id(0)
    rows = 8 * STEP
    index = col_ref[...]
    r, slot, odd, imag = sublane_roles(rows)
    lane = iota((rows, 128), 1)
    half = lane >> 6
    chosen = (lane == (index >> 1)).astype(F32).astype(BF16)
    both = matmul(chosen, prior_ref[...])
    v = jnp.where(imag == 1, both[:, 128:], both[:, :128])
    v = jnp.where((index & 1) == odd, v, pltpu.roll(v, 64, 1))
    v = jnp.where(half == odd, v, 0.0)
    f = lax.dot_general(
        v.reshape(STEP, 8, 128).astype(BF16),
        w_ref[...],
        (((2,), (2,)), ((0,), (0,))),
        preferred_element_type=F32,
    ).reshape(rows, 64)
    f = jnp.concatenate([f, f], axis=1)
    f = jnp.where((lane & 1) == slot, f, 0.0)
    f = shift_lanes(f, odd - slot)
    f = jnp.where(half == ((r >> 3) & 1), f, 0.0)
    f = jnp.concatenate([jnp.where(imag == 0, f, 0.0), jnp.where(imag == 1, f, 0.0)], axis=1)
    gather = (iota((16, rows), 1) >> 4 == iota((16, rows), 0)).astype(F32).astype(BF16)
    high, low = high_low(f)
    acc_ref[pl.ds(pl.multiple_of(step * 16, 16), 16), :] = matmul(gather, high) + matmul(gather, low)

    @pl.when(step == pl.num_programs(0) - 1)
    def _():
        moved = (cur_ref[...].astype(F32) + acc_ref[...]).astype(BF16)
        turned = matmul(depth_major(), moved).astype(BF16).reshape(share, 128 // share, 256)
        for g in range(16 // share):
            out_ref[g * share : (g + 1) * share] = turned


def adjoint_kernel(share, col_ref, row_ref, w_ref, parts_ref, grad_ref, pulled_ref, image_ref, acc_ref):
    step = pl.program_id(0)
    rows = 8 * STEP

    @pl.when(step == 0)
    def _():
        total = parts_ref[0:share].astype(F32)
        for g in range(1, 16 // share):
            total = total + parts_ref[g * share : (g + 1) * share].astype(F32)
        total = total.reshape(128, 256)
        frm, to = iota((128, 128), 1), iota((128, 128), 0)
        turn = ((frm & 15) * Z + (frm >> 4) == to).astype(F32).astype(BF16)
        high, low = high_low(total)
        lowest = (total - high.astype(F32) - low.astype(F32)).astype(BF16)
        grad = matmul(turn, high) + matmul(turn, low) + matmul(turn, lowest)
        grad_ref[...] = grad
        image_ref[...] = grad.astype(BF16)
        acc_ref[...] = jnp.zeros_like(acc_ref)

    index = col_ref[...]
    r, slot, odd, imag = sublane_roles(rows)
    lane = iota((rows, 128), 1)
    half = lane >> 6
    chosen = (lane == step * (STEP // 2) + (r >> 4)).astype(F32).astype(BF16)
    both = matmul(chosen, image_ref[...])
    v = jnp.where(imag == 1, both[:, 128:], both[:, :128])
    v = jnp.where(half == ((r >> 3) & 1), v, pltpu.roll(v, 64, 1))
    v = jnp.where((lane & 1) == odd, v, 0.0)
    v = shift_lanes(v, slot - odd)
    f = lax.dot_general(
        v[:, :64].reshape(STEP, 8, 64).astype(BF16),
        w_ref[...],
        (((2,), (1,)), ((0,), (0,))),
        preferred_element_type=F32,
    ).reshape(rows, 128)
    f = jnp.where(half == odd, f, 0.0)
    f = f + pltpu.roll(f, 64, 1)
    f = jnp.where(half == (index & 1), f, 0.0)
    f = jnp.concatenate([jnp.where(imag == 0, f, 0.0), jnp.where(imag == 1, f, 0.0)], axis=1)
    scatter = (iota((128, rows), 0) == (row_ref[...] >> 1)).astype(F32).astype(BF16)
    high, low = high_low(f)
    acc_ref[...] += matmul(scatter, high) + matmul(scatter, low)

    @pl.when(step == pl.num_programs(0) - 1)
    def _():
        pulled_ref[...] = acc_ref[...].astype(BF16)


def data_kernel(moved_ref, sens_ref, data_ref, mask_ref, row_ref, back_ref, table_ref, out_ref, acc_ref):
    chunk = pl.program_id(1)
    moved = moved_ref[...].reshape(NY, 256).astype(F32)
    image_re, image_im = moved[:, :NX], moved[:, NX:]
    mask = mask_ref[...].astype(F32)
    table = table_ref[...]
    sens_re, sens_im, images = [], [], []
    for c in range(PAIR):
        sens = sens_ref[:, c].reshape(NY, 256).astype(F32)
        sens_re.append(sens[:, :NX])
        sens_im.append(sens[:, NX:])
        images.append(sens_re[c] * image_re - sens_im[c] * image_im)
        images.append(sens_re[c] * image_im + sens_im[c] * image_re)
    images = [jnp.concatenate(images[2 * c : 2 * c + 2], axis=1).astype(BF16) for c in range(PAIR)]
    spectra = matmul(jnp.concatenate(images, axis=0), row_ref[...])
    tops, bottoms = [], []
    for c in range(PAIR):
        s = spectra[c * NY : (c + 1) * NY]
        tops.append(s)
        bottoms += [s[:, NX:], -s[:, :NX]]
    stacked = jnp.concatenate([jnp.concatenate(tops, axis=1), jnp.concatenate(bottoms, axis=1)], axis=0).astype(BF16)
    spectra = matmul(table, stacked)
    tops, bottoms = [], []
    for c in range(PAIR):
        measured = data_ref[c].reshape(NY, 256).astype(F32)
        s = spectra[:, c * 256 : (c + 1) * 256] - measured
        res_re, res_im = mask * s[:, :NX], mask * s[:, NX:]
        tops += [res_re, res_im]
        bottoms += [-res_im, res_re]
    stacked = jnp.concatenate([jnp.concatenate(tops, axis=1), jnp.concatenate(bottoms, axis=1)], axis=0).astype(BF16)
    columns = matmul(table, stacked).astype(BF16)
    rows = matmul(jnp.concatenate([columns[:, c * 256 : (c + 1) * 256] for c in range(PAIR)], axis=0), back_ref[...])
    real = imag = 0.0
    for c in range(PAIR):
        b = rows[c * NY : (c + 1) * NY]
        back_re, back_im = b[:, :NX], b[:, NX:]
        real += sens_re[c] * back_re + sens_im[c] * back_im
        imag += sens_re[c] * back_im - sens_im[c] * back_re
    both = jnp.concatenate([real, imag], axis=1)
    total = jnp.where(chunk == 0, both, acc_ref[...] + both)
    acc_ref[...] = total
    out_ref[...] = total.astype(BF16).reshape(out_ref.shape)


def full(shape):
    return pl.BlockSpec(shape, lambda *_: (0,) * len(shape))


def warp_forward(share, columns, weights, prior, current):
    return pl.pallas_call(
        functools.partial(warp_kernel, share),
        grid=(256 // STEP,),
        in_specs=[
            pl.BlockSpec((8 * STEP, 1), lambda i: (i, 0)),
            pl.BlockSpec((STEP, 64, 128), lambda i: (i, 0, 0)),
            full((128, 256)),
            full((128, 256)),
        ],
        out_specs=full((16, 128 // share, 256)),
        out_shape=jax.ShapeDtypeStruct((16, 128 // share, 256), BF16),
        scratch_shapes=[pltpu.VMEM((128, 256), F32)],
        compiler_params=pltpu.CompilerParams(vmem_limit_bytes=32 * 2**20),
        name="warp_forward",
    )(columns, weights, prior, current)


def warp_adjoint(share, columns, rows, weights, parts):
    return pl.pallas_call(
        functools.partial(adjoint_kernel, share),
        grid=(256 // STEP,),
        in_specs=[
            pl.BlockSpec((8 * STEP, 1), lambda i: (i, 0)),
            pl.BlockSpec((1, 8 * STEP), lambda i: (0, i)),
            pl.BlockSpec((STEP, 64, 128), lambda i: (i, 0, 0)),
            full((16, 128 // share, 256)),
        ],
        out_specs=[full((128, 256)), full((128, 256))],
        out_shape=[jax.ShapeDtypeStruct((128, 256), F32), jax.ShapeDtypeStruct((128, 256), BF16)],
        scratch_shapes=[pltpu.VMEM((128, 256), BF16), pltpu.VMEM((128, 256), F32)],
        compiler_params=pltpu.CompilerParams(vmem_limit_bytes=32 * 2**20),
        name="warp_adjoint",
    )(columns, rows, weights, parts)


def data_gradient(share, moved, sens, measured, mask):
    depths, coils = Z // share, 2 * share
    matrix = row_matrix()
    return pl.pallas_call(
        data_kernel,
        grid=(depths, coils // PAIR),
        in_specs=[
            pl.BlockSpec((16, 1, 16, 256), lambda z, c: (0, z, 0, 0)),
            pl.BlockSpec((16, PAIR, 1, 16, 256), lambda z, c: (0, c, z, 0, 0)),
            pl.BlockSpec((PAIR, 1, NY, 256), lambda z, c: (c, z, 0, 0)),
            full((NY, NX)),
            full((256, 256)),
            full((256, 256)),
            full((NY, 2 * NY)),
        ],
        out_specs=pl.BlockSpec((16, 1, 16, 256), lambda z, c: (0, z, 0, 0)),
        out_shape=jax.ShapeDtypeStruct((16, depths, 16, 256), BF16),
        scratch_shapes=[pltpu.VMEM((NY, 256), F32)],
        compiler_params=pltpu.CompilerParams(vmem_limit_bytes=32 * 2**20),
        name="data_gradient",
    )(moved, sens, measured, mask, jnp.asarray(matrix), jnp.asarray(matrix.T), jnp.asarray(column_table()))


def on_device(share, cine_image, warp_blocks, warp_index, sample_mask, kspace_data, sensitivity):
    coil = ("group", "member")
    groups, depths = 16 // share, Z // share
    loop = 16
    forward = [(i, (i + 1) % loop) for i in range(loop)]
    backward = [((i + 1) % loop, i) for i in range(loop)]
    current = cine_image.reshape(128, 256)
    prior = lax.ppermute(current, "bin", forward)

    measured = kspace_data[0].reshape(2, NY, share, depths, 256).transpose(2, 0, 3, 1, 4)
    if share > 1:
        measured = lax.all_to_all(measured, "member", 0, 0, tiled=True)
    measured = measured.reshape(2 * share, depths, NY, 256)
    sens = sensitivity.reshape(groups, 2 * share, 16, share, depths, 256).transpose(0, 3, 1, 4, 2, 5)
    sens = sens.reshape(16, 2 * share, depths, 16, 256)
    sens = lax.all_to_all(sens, coil, 0, 0, tiled=True)

    weights = warp_blocks.reshape(256, 2, 32, 128).transpose(0, 2, 1, 3).reshape(256, 64, 128)
    index = warp_index[0] - lax.axis_index(coil) * 256
    index = jnp.broadcast_to(index[:, :, None], (256, 2, 4)).reshape(2048)
    moved = warp_forward(share, index.reshape(2048, 1), weights, prior, current)
    moved = lax.all_to_all(moved, coil, 0, 0, tiled=True).reshape(16, depths, 16, 256)
    parts = data_gradient(share, moved, sens, measured, sample_mask[0])
    parts = lax.all_to_all(parts, coil, 0, 0, tiled=True).reshape(16, 128 // share, 256)
    grad, pulled = warp_adjoint(share, index.reshape(2048, 1), index.reshape(1, 2048), weights, parts)
    from_next = lax.ppermute(pulled, "bin", backward)
    return (grad + from_next.astype(F32)).reshape(1, 16, Z, 256)


def solution(mesh):
    share = SHARE
    inner = Mesh(mesh.devices.reshape(16, 16 // share, share), ("bin", "group", "member"))
    coil = ("group", "member")
    return jax.shard_map(
        functools.partial(on_device, share),
        mesh=inner,
        in_specs=(
            P("bin", coil, None, None),
            P("bin", coil, None, None),
            P("bin", coil, None),
            P("bin", None, None),
            P("bin", coil, None, None, None),
            P(None, coil, None, None),
        ),
        out_specs=P("bin", coil, None, None),
        check_vma=False,
    )
```

```python
import jax
import jax.numpy as jnp
import numpy as np
from jax import lax
from jax.experimental import pallas as pl
from jax.experimental.pallas import tpu as pltpu
from jax.sharding import Mesh
from jax.sharding import PartitionSpec as P

NY = 256
NX = 128
Z = 8
SHARE = 4
PAIR = 4
STEP = 128

VMEM = 60 * 2**20

F32 = jnp.float32
BF16 = jnp.bfloat16


def cosine_sine(length):
    positions = np.arange(length)
    phases = positions[:, None] * positions[None, :] % length
    angles = phases * (2.0 * np.pi / length)
    return np.cos(angles) / np.sqrt(length), np.sin(angles) / np.sqrt(length)


def row_matrix():
    cosine, sine = cosine_sine(NX)
    return np.block([[cosine, -sine], [sine, cosine]]).astype(BF16)


def column_table():
    return np.concatenate(cosine_sine(NY), axis=1).astype(BF16)


def iota(shape, axis):
    return lax.broadcasted_iota(jnp.int32, shape, axis)


def matmul(a, b):
    return jnp.dot(a, b, preferred_element_type=F32)


def high_low(values):
    high = values.astype(BF16)
    return high, (values - high.astype(F32)).astype(BF16)


def sublane_roles(rows):
    r = iota((rows, 128), 0)
    return r, (r >> 2) & 1, (r >> 1) & 1, r & 1


def shift_lanes(values, distance):
    return jnp.where(
        distance == 1,
        pltpu.roll(values, 1, 1),
        jnp.where(distance == -1, pltpu.roll(values, 127, 1), values),
    )


def as_matrix(condition):
    return condition.astype(F32).astype(BF16)


def depth_major(core):
    to, frm = iota((128, 128), 0), iota((128, 128), 1)
    return as_matrix((to & 15) * Z + ((to >> 4) ^ core) == frm)


def warp_kernel(place_ref, col_ref, w_ref, prior_ref, cur_ref, out_ref, acc_ref):
    step = pl.program_id(0)
    rows = 8 * STEP
    index = col_ref[...]
    r, slot, odd, imag = sublane_roles(rows)
    lane = iota((rows, 128), 1)
    half = lane >> 6
    chosen = (lane == (index >> 1)).astype(F32).astype(BF16)
    both = matmul(chosen, prior_ref[...])
    v = jnp.where(imag == 1, both[:, 128:], both[:, :128])
    v = jnp.where((index & 1) == odd, v, pltpu.roll(v, 64, 1))
    v = jnp.where(half == odd, v, 0.0)
    f = lax.dot_general(
        v.reshape(STEP // 4, 32, 128).astype(BF16),
        w_ref[...].reshape(STEP // 4, 256, 128),
        (((2,), (2,)), ((0,), (0,))),
        preferred_element_type=F32,
    ).reshape(rows, 256)
    f = jnp.where(((r >> 4) & 1) == 0, f[:, :128], f[:, 128:])
    f = jnp.where(((lane & 1) == slot) & (half == ((r >> 3) & 1)), f, 0.0)
    f = shift_lanes(f, odd - slot)
    f = jnp.concatenate([jnp.where(imag == 0, f, 0.0), jnp.where(imag == 1, f, 0.0)], axis=1)
    lines = STEP // 2
    gather = as_matrix(iota((lines, rows), 1) >> 4 == iota((lines, rows), 0))
    high, low = high_low(f)
    acc_ref[pl.ds(pl.multiple_of(step * lines, lines), lines), :] = matmul(gather, high) + matmul(gather, low)

    @pl.when(step == pl.num_programs(0) - 1)
    def _():
        moved = (cur_ref[...].astype(F32) + acc_ref[...]).astype(BF16)
        turned = matmul(depth_major(place_ref[1]), moved).astype(BF16).reshape(SHARE, 128 // SHARE, 256)
        for g in range(16 // SHARE):
            out_ref[g * SHARE : (g + 1) * SHARE] = turned


def adjoint_kernel(place_ref, col_ref, row_ref, w_ref, parts_ref, grad_ref, pulled_ref, image_ref, acc_ref):
    step = pl.program_id(0)
    rows = 8 * STEP

    @pl.when(step == 0)
    def _():
        total = parts_ref[0:SHARE].astype(F32)
        for g in range(1, 16 // SHARE):
            total = total + parts_ref[g * SHARE : (g + 1) * SHARE].astype(F32)
        total = total.reshape(128, 256)
        frm, to = iota((128, 128), 1), iota((128, 128), 0)
        turn = as_matrix((frm & 15) * Z + ((frm >> 4) ^ place_ref[1]) == to)
        high, low = high_low(total)
        lowest = (total - high.astype(F32) - low.astype(F32)).astype(BF16)
        grad = matmul(turn, high) + matmul(turn, low) + matmul(turn, lowest)
        grad_ref[...] = grad
        image_ref[...] = grad.astype(BF16)
        acc_ref[...] = jnp.zeros_like(acc_ref)

    index = col_ref[...]
    r, slot, odd, imag = sublane_roles(rows)
    lane = iota((rows, 128), 1)
    half = lane >> 6
    chosen = (lane == step * (STEP // 2) + (r >> 4)).astype(F32).astype(BF16)
    both = matmul(chosen, image_ref[...])
    v = jnp.where(imag == 1, both[:, 128:], both[:, :128])
    v = jnp.where(half == ((r >> 3) & 1), v, pltpu.roll(v, 64, 1))
    v = jnp.where((lane & 1) == odd, v, 0.0)
    v = shift_lanes(v, slot - odd)
    place4 = (r >> 3) & 3
    v = jnp.concatenate([jnp.where(half == place4, v, 0.0), jnp.where(half + 2 == place4, v, 0.0)], axis=1)
    f = lax.dot_general(
        v.reshape(STEP // 4, 32, 256).astype(BF16),
        w_ref[...].reshape(STEP // 4, 256, 128),
        (((2,), (1,)), ((0,), (0,))),
        preferred_element_type=F32,
    ).reshape(rows, 128)
    f = jnp.where(half == odd, f, 0.0)
    f = f + pltpu.roll(f, 64, 1)
    f = jnp.where(half == (index & 1), f, 0.0)
    f = jnp.concatenate([jnp.where(imag == 0, f, 0.0), jnp.where(imag == 1, f, 0.0)], axis=1)
    scatter = (iota((128, rows), 0) == (row_ref[...] >> 1)).astype(F32).astype(BF16)
    high, low = high_low(f)
    acc_ref[...] += matmul(scatter, high) + matmul(scatter, low)

    @pl.when(step == pl.num_programs(0) - 1)
    def _():
        pulled_ref[...] = acc_ref[...].astype(BF16)


def data_kernel(
    place_ref,
    moved_ref,
    own_ref,
    other_ref,
    data0_ref,
    data1_ref,
    data2_ref,
    data3_ref,
    mask_ref,
    row_ref,
    back_ref,
    table_ref,
    out_ref,
    acc_ref,
):
    depth, chunk = pl.program_id(0), pl.program_id(1)
    moved = moved_ref[...].reshape(NY, 256).astype(F32)
    image_re, image_im = moved[:, :NX], moved[:, NX:]
    mask = mask_ref[...].astype(F32)
    table = table_ref[...]
    sens_re, sens_im, images = [], [], []
    for c in range(PAIR):
        sens = jnp.where(depth == 0, own_ref[c // 2, :, c % 2], other_ref[c // 2, :, c % 2])
        sens = sens.reshape(NY, 256).astype(F32)
        sens_re.append(sens[:, :NX])
        sens_im.append(sens[:, NX:])
        re = sens_re[c] * image_re - sens_im[c] * image_im
        im = sens_re[c] * image_im + sens_im[c] * image_re
        images.append(jnp.concatenate([re, im], axis=1).astype(BF16))
    spectra = matmul(jnp.concatenate(images, axis=0), row_ref[...])
    tops, bottoms = [], []
    for c in range(PAIR):
        s = spectra[c * NY : (c + 1) * NY]
        tops.append(s)
        bottoms += [s[:, NX:], -s[:, :NX]]
    stacked = jnp.concatenate([jnp.concatenate(tops, axis=1), jnp.concatenate(bottoms, axis=1)], axis=0).astype(BF16)
    spectra = matmul(table, stacked)
    tops, bottoms = [], []
    for c in range(PAIR):
        source = place_ref[3 + chunk * (PAIR // 2) + c // 2]
        low = jnp.where(source == 0, data0_ref[c % 2, 0], data1_ref[c % 2, 0])
        high = jnp.where(source == 2, data2_ref[c % 2, 0], data3_ref[c % 2, 0])
        measured = jnp.where(source < 2, low, high).astype(F32)
        s = spectra[:, c * 256 : (c + 1) * 256] - measured
        res_re, res_im = mask * s[:, :NX], mask * s[:, NX:]
        tops += [res_re, res_im]
        bottoms += [-res_im, res_re]
    stacked = jnp.concatenate([jnp.concatenate(tops, axis=1), jnp.concatenate(bottoms, axis=1)], axis=0).astype(BF16)
    columns = matmul(table, stacked).astype(BF16)
    rows = jnp.concatenate([columns[:, c * 256 : (c + 1) * 256] for c in range(PAIR)], axis=0)
    rows = matmul(rows, back_ref[...])
    real = imag = 0.0
    for c in range(PAIR):
        b = rows[c * NY : (c + 1) * NY]
        back_re, back_im = b[:, :NX], b[:, NX:]
        real += sens_re[c] * back_re + sens_im[c] * back_im
        imag += sens_re[c] * back_im - sens_im[c] * back_re
    both = jnp.concatenate([real, imag], axis=1)
    total = jnp.where(chunk == 0, both, acc_ref[...] + both)
    acc_ref[...] = total
    out_ref[...] = total.astype(BF16).reshape(out_ref.shape)


def pick_kernel(place_ref, sens_ref, out_ref):
    to, frm = iota((64, 128), 0), iota((64, 128), 1)
    turn = as_matrix((to & 15) * Z + (to >> 4) * 2 + place_ref[1] == frm)
    for g in range(16 // SHARE):
        for c in range(2):
            picked = matmul(turn, sens_ref[g, 0, c]).astype(BF16)
            out_ref[g * SHARE : (g + 1) * SHARE, c] = picked.reshape(SHARE, 16, 256)


def turn_kernel(place_ref, data_ref, *out_refs):
    to, frm = iota((128, 128), 0), iota((128, 128), 1)
    depth = (((to >> 5) ^ place_ref[2]) << 1) + (((to >> 4) & 1) ^ place_ref[1])
    turn = as_matrix((to & 15) * Z + depth == frm)
    for b in range(data_ref.shape[1]):
        turned = matmul(turn, data_ref[0, b]).astype(BF16).reshape(SHARE, 2, 16, 256)
        for j in range(SHARE):
            out_refs[j][0, :, b * 16 : (b + 1) * 16] = turned[j]


def full(shape):
    return pl.BlockSpec(shape, lambda *_: (0,) * len(shape))


def call(kernel, place, arrays, grid, in_specs, out_specs, out_shape, scratch, name, micros):
    return pl.pallas_call(
        kernel,
        grid_spec=pltpu.PrefetchScalarGridSpec(
            num_scalar_prefetch=1, grid=grid, in_specs=in_specs, out_specs=out_specs, scratch_shapes=scratch
        ),
        out_shape=out_shape,
        compiler_params=pltpu.CompilerParams(vmem_limit_bytes=VMEM),
        cost_estimate=pl.CostEstimate(flops=0, bytes_accessed=int(micros * 3e6), transcendentals=0),
        name=name,
    )(place, *arrays)


def warp_forward(place, columns, weights, prior, current):
    shape = (16, 128 // SHARE, 256)
    return call(
        warp_kernel,
        place,
        (columns, weights, prior, current),
        (256 // STEP,),
        [
            pl.BlockSpec((8 * STEP, 1), lambda i, p: (i, 0)),
            pl.BlockSpec((STEP, 64, 128), lambda i, p: (i, 0, 0)),
            full((128, 256)),
            full((128, 256)),
        ],
        full(shape),
        jax.ShapeDtypeStruct(shape, BF16),
        [pltpu.VMEM((128, 256), F32)],
        "warp_forward",
        8,
    )


def warp_adjoint(place, columns, rows, weights, parts):
    return call(
        adjoint_kernel,
        place,
        (columns, rows, weights, parts),
        (256 // STEP,),
        [
            pl.BlockSpec((8 * STEP, 1), lambda i, p: (i, 0)),
            pl.BlockSpec((1, 8 * STEP), lambda i, p: (0, i)),
            pl.BlockSpec((STEP, 64, 128), lambda i, p: (i, 0, 0)),
            full((16, 128 // SHARE, 256)),
        ],
        [full((128, 256)), full((128, 256))],
        [jax.ShapeDtypeStruct((128, 256), F32), jax.ShapeDtypeStruct((128, 256), BF16)],
        [pltpu.VMEM((128, 256), BF16), pltpu.VMEM((128, 256), F32)],
        "warp_adjoint",
        8,
    )


def data_gradient(place, moved, own, other, measured, mask):
    matrix = row_matrix()
    last = 8 // PAIR - 1
    sens_block = (PAIR // 2, 16, 2, 16, 256)
    return call(
        data_kernel,
        place,
        (moved, own, other, *measured, mask, jnp.asarray(matrix), jnp.asarray(matrix.T), jnp.asarray(column_table())),
        (2, 8 // PAIR),
        [
            pl.BlockSpec((16, 1, 16, 256), lambda z, c, p: (0, z, 0, 0)),
            pl.BlockSpec(sens_block, lambda z, c, p: (jnp.where(z == 0, c, last), 0, 0, 0, 0)),
            pl.BlockSpec(sens_block, lambda z, c, p: (jnp.where(z == 0, 0, c), 0, 0, 0, 0)),
            *[pl.BlockSpec((2, 1, NY, 256), lambda z, c, p: (0, z, 0, 0))] * 4,
            full((NY, NX)),
            full((256, 256)),
            full((256, 256)),
            full((NY, 2 * NY)),
        ],
        pl.BlockSpec((16, 1, 16, 256), lambda z, c, p: (0, z, 0, 0)),
        jax.ShapeDtypeStruct((16, 2, 16, 256), BF16),
        [pltpu.VMEM((NY, 256), F32)],
        "data_gradient",
        8,
    )


def pick_share(place, sensitivity):
    return call(
        pick_kernel,
        place,
        (sensitivity.reshape(4, 4, 2, 128, 256),),
        (1,),
        [pl.BlockSpec((4, 1, 2, 128, 256), lambda g, p: (0, p[0], 0, 0, 0))],
        full((16, 2, 16, 256)),
        jax.ShapeDtypeStruct((16, 2, 16, 256), BF16),
        [],
        "pick_share",
        1,
    )


def turn_data(place, data):
    blocks = 8
    return call(
        turn_kernel,
        place,
        (data.reshape(2, 16, 128, 256),),
        (2, 16 // blocks),
        [pl.BlockSpec((1, blocks, 128, 256), lambda c, b, p: (c, b, 0, 0))],
        [pl.BlockSpec((1, 2, 16 * blocks, 256), lambda c, b, p: (c, 0, b, 0))] * SHARE,
        [jax.ShapeDtypeStruct((2, 2, NY, 256), BF16)] * SHARE,
        [],
        "turn_data",
        3,
    )


def on_device(cine_image, warp_blocks, warp_index, sample_mask, kspace_data, sensitivity):
    loop_axes, coil = ("y", "half", "core"), ("group", "member")
    row, core, member = lax.axis_index("y"), lax.axis_index("core"), lax.axis_index("member")
    offsets = (0, 1, -1, 2)
    place = jnp.stack([row, core, member, *[((row + d) % 4) ^ member for d in offsets]])
    forward = [(i, (i + 1) % 16) for i in range(16)]
    backward = [((i + 1) % 16, i) for i in range(16)]
    current = cine_image.reshape(128, 256)
    prior = lax.ppermute(current, loop_axes, forward)

    sens, prior, kspace_data = lax.optimization_barrier((pick_share(place, sensitivity), prior, kspace_data))
    sens = lax.all_to_all(sens, coil, 0, 0, tiled=True)
    measured = turn_data(place, kspace_data)
    measured = [
        piece if j == 0 else lax.ppermute(piece, "member", [(i, i ^ j) for i in range(SHARE)])
        for j, piece in enumerate(measured)
    ]

    weights = warp_blocks.reshape(256, 2, 32, 128).transpose(0, 2, 1, 3).reshape(256, 64, 128)
    index = warp_index[0] - lax.axis_index(coil) * 256
    index = jnp.broadcast_to(index[:, :, None], (256, 2, 4)).reshape(2048)
    columns, rows = index.reshape(2048, 1), index.reshape(1, 2048)
    prior, sens, measured[0] = lax.optimization_barrier((prior, sens, measured[0]))
    moved = warp_forward(place, columns, weights, prior, current)
    sens = [sens] + [lax.ppermute(sens, "y", [(i, (i - d) % 4) for i in range(4)]) for d in offsets[1:]]
    moved, sens, measured[1], measured[2] = lax.optimization_barrier((moved, sens, measured[1], measured[2]))
    moved = lax.all_to_all(moved, coil, 0, 0, tiled=True).reshape(16, 2, 16, 256)
    sens = jnp.stack(sens)
    other = lax.ppermute(sens, "core", [(0, 1), (1, 0)])
    parts = data_gradient(place, moved, sens, other, measured, sample_mask[0])
    parts = lax.all_to_all(parts, coil, 0, 0, tiled=True).reshape(16, 32, 256)
    grad, pulled = warp_adjoint(place, columns, rows, weights, parts)
    from_next = lax.ppermute(pulled, loop_axes, backward)
    return (grad + from_next.astype(F32)).reshape(1, 16, Z, 256)


def solution(mesh):
    inner = Mesh(mesh.devices.reshape(4, 2, 2, 16 // SHARE, SHARE), ("y", "half", "core", "group", "member"))
    bins, coil = ("y", "half", "core"), ("group", "member")
    return jax.shard_map(
        on_device,
        mesh=inner,
        in_specs=(
            P(bins, coil, None, None),
            P(bins, coil, None, None),
            P(bins, coil, None),
            P(bins, None, None),
            P(bins, coil, None, None, None),
            P(None, coil, None, None),
        ),
        out_specs=P(bins, coil, None, None),
        check_vma=False,
    )
```

```python
import jax
import jax.numpy as jnp
import numpy as np
from jax import lax
from jax.experimental import pallas as pl
from jax.experimental.pallas import tpu as pltpu
from jax.sharding import Mesh
from jax.sharding import PartitionSpec as P

NY = 256
NX = 128
Z = 8
SHARE = 4
PAIR = 8
STEP = 128

F32 = jnp.float32
BF16 = jnp.bfloat16


def cosine_sine(length):
    positions = np.arange(length)
    phases = positions[:, None] * positions[None, :] % length
    angles = phases * (2.0 * np.pi / length)
    return np.cos(angles) / np.sqrt(length), np.sin(angles) / np.sqrt(length)


def row_matrix():
    cosine, sine = cosine_sine(NX)
    return np.block([[cosine, -sine], [sine, cosine]]).astype(BF16)


def column_table():
    return np.concatenate(cosine_sine(NY), axis=1).astype(BF16)


def iota(shape, axis):
    return lax.broadcasted_iota(jnp.int32, shape, axis)


def matmul(a, b):
    return jnp.dot(a, b, preferred_element_type=F32)


def high_low(values):
    high = values.astype(BF16)
    return high, (values - high.astype(F32)).astype(BF16)


def sublane_roles(rows):
    r = iota((rows, 128), 0)
    return r, (r >> 2) & 1, (r >> 1) & 1, r & 1


def shift_lanes(values, distance):
    return jnp.where(
        distance == 1,
        pltpu.roll(values, 1, 1),
        jnp.where(distance == -1, pltpu.roll(values, 127, 1), values),
    )


def as_matrix(condition):
    return condition.astype(F32).astype(BF16)


def depth_major(core):
    to, frm = iota((128, 128), 0), iota((128, 128), 1)
    return as_matrix((to & 15) * Z + ((to >> 4) ^ core) == frm)


def fetches(w_ref, slot_ref, sems):
    return [
        pltpu.make_async_copy(w_ref.at[pl.ds(i * STEP, STEP)], slot_ref.at[i], sems.at[i]) for i in range(256 // STEP)
    ]


def wait_for(step, copies):
    for i, copy in enumerate(copies):
        pl.when(step == i)(copy.wait)


def warp_kernel(place_ref, col_ref, w_ref, prior_ref, cur_ref, out_ref, acc_ref, slot_ref, sems):
    step = pl.program_id(0)
    copies = fetches(w_ref, slot_ref, sems)

    @pl.when(step == 0)
    def _():
        for copy in copies:
            copy.start()

    rows = 8 * STEP
    index = col_ref[...]
    r, slot, odd, imag = sublane_roles(rows)
    lane = iota((rows, 128), 1)
    half = lane >> 6
    chosen = (lane == (index >> 1)).astype(F32).astype(BF16)
    both = matmul(chosen, prior_ref[...])
    v = jnp.where(imag == 1, both[:, 128:], both[:, :128])
    v = jnp.where((index & 1) == odd, v, pltpu.roll(v, 64, 1))
    v = jnp.where(half == odd, v, 0.0)
    wait_for(step, copies)
    f = lax.dot_general(
        v.reshape(STEP // 4, 32, 128).astype(BF16),
        slot_ref[step].reshape(STEP // 4, 256, 128),
        (((2,), (2,)), ((0,), (0,))),
        preferred_element_type=F32,
    ).reshape(rows, 256)
    f = jnp.where(((r >> 4) & 1) == 0, f[:, :128], f[:, 128:])
    f = jnp.where(((lane & 1) == slot) & (half == ((r >> 3) & 1)), f, 0.0)
    f = shift_lanes(f, odd - slot)
    f = jnp.concatenate([jnp.where(imag == 0, f, 0.0), jnp.where(imag == 1, f, 0.0)], axis=1)
    lines = STEP // 2
    gather = as_matrix(iota((lines, rows), 1) >> 4 == iota((lines, rows), 0))
    high, low = high_low(f)
    acc_ref[pl.ds(pl.multiple_of(step * lines, lines), lines), :] = matmul(gather, high) + matmul(gather, low)

    @pl.when(step == pl.num_programs(0) - 1)
    def _():
        moved = (cur_ref[...].astype(F32) + acc_ref[...]).astype(BF16)
        turned = matmul(depth_major(place_ref[1]), moved).astype(BF16).reshape(SHARE, 128 // SHARE, 256)
        for g in range(16 // SHARE):
            out_ref[g * SHARE : (g + 1) * SHARE] = turned


def adjoint_kernel(place_ref, col_ref, row_ref, w_ref, parts_ref, grad_ref, pulled_ref, image_ref, acc_ref, slot_ref, sems):
    step = pl.program_id(0)
    copies = fetches(w_ref, slot_ref, sems)
    rows = 8 * STEP

    @pl.when(step == 0)
    def _():
        for copy in copies:
            copy.start()
        total = parts_ref[0:SHARE].astype(F32)
        for g in range(1, 16 // SHARE):
            total = total + parts_ref[g * SHARE : (g + 1) * SHARE].astype(F32)
        total = total.reshape(128, 256)
        frm, to = iota((128, 128), 1), iota((128, 128), 0)
        turn = as_matrix((frm & 15) * Z + ((frm >> 4) ^ place_ref[1]) == to)
        high, low = high_low(total)
        lowest = (total - high.astype(F32) - low.astype(F32)).astype(BF16)
        grad = matmul(turn, high) + matmul(turn, low) + matmul(turn, lowest)
        grad_ref[...] = grad
        image_ref[...] = grad.astype(BF16)
        acc_ref[...] = jnp.zeros_like(acc_ref)

    index = col_ref[...]
    r, slot, odd, imag = sublane_roles(rows)
    lane = iota((rows, 128), 1)
    half = lane >> 6
    chosen = (lane == step * (STEP // 2) + (r >> 4)).astype(F32).astype(BF16)
    both = matmul(chosen, image_ref[...])
    v = jnp.where(imag == 1, both[:, 128:], both[:, :128])
    v = jnp.where(half == ((r >> 3) & 1), v, pltpu.roll(v, 64, 1))
    v = jnp.where((lane & 1) == odd, v, 0.0)
    v = shift_lanes(v, slot - odd)
    place4 = (r >> 3) & 3
    v = jnp.concatenate([jnp.where(half == place4, v, 0.0), jnp.where(half + 2 == place4, v, 0.0)], axis=1)
    wait_for(step, copies)
    f = lax.dot_general(
        v.reshape(STEP // 4, 32, 256).astype(BF16),
        slot_ref[step].reshape(STEP // 4, 256, 128),
        (((2,), (1,)), ((0,), (0,))),
        preferred_element_type=F32,
    ).reshape(rows, 128)
    f = jnp.where(half == odd, f, 0.0)
    f = f + pltpu.roll(f, 64, 1)
    f = jnp.where(half == (index & 1), f, 0.0)
    f = jnp.concatenate([jnp.where(imag == 0, f, 0.0), jnp.where(imag == 1, f, 0.0)], axis=1)
    scatter = (iota((128, rows), 0) == (row_ref[...] >> 1)).astype(F32).astype(BF16)
    high, low = high_low(f)
    acc_ref[...] += matmul(scatter, high) + matmul(scatter, low)

    @pl.when(step == pl.num_programs(0) - 1)
    def _():
        pulled_ref[...] = acc_ref[...].astype(BF16)


def data_kernel(
    place_ref,
    moved_ref,
    own0_ref,
    own1_ref,
    own2_ref,
    own3_ref,
    other0_ref,
    other1_ref,
    other2_ref,
    other3_ref,
    data0_ref,
    data1_ref,
    data2_ref,
    data3_ref,
    mask_ref,
    tables_ref,
    out_ref,
    acc_ref,
):
    own_refs = (own0_ref, own1_ref, own2_ref, own3_ref)
    other_refs = (other0_ref, other1_ref, other2_ref, other3_ref)
    depth, chunk = pl.program_id(0), pl.program_id(1)
    moved = moved_ref[...].reshape(NY, 256).astype(F32)
    image_re, image_im = moved[:, :NX], moved[:, NX:]
    mask = mask_ref[...].astype(F32)
    row_table, back_table, table = tables_ref[:, :256], tables_ref[:, 256:512], tables_ref[:, 512:]
    sens_re, sens_im, images = [], [], []
    for c in range(PAIR):
        sens = jnp.where(depth == 0, own_refs[c // 2][:, c % 2], other_refs[c // 2][:, c % 2])
        sens = sens.reshape(NY, 256).astype(F32)
        sens_re.append(sens[:, :NX])
        sens_im.append(sens[:, NX:])
        re = sens_re[c] * image_re - sens_im[c] * image_im
        im = sens_re[c] * image_im + sens_im[c] * image_re
        images.append(jnp.concatenate([re, im], axis=1).astype(BF16))
    spectra = matmul(jnp.concatenate(images, axis=0), row_table)
    tops, bottoms = [], []
    for c in range(PAIR):
        s = spectra[c * NY : (c + 1) * NY]
        tops.append(s)
        bottoms += [s[:, NX:], -s[:, :NX]]
    stacked = jnp.concatenate([jnp.concatenate(tops, axis=1), jnp.concatenate(bottoms, axis=1)], axis=0).astype(BF16)
    spectra = matmul(table, stacked)
    tops, bottoms = [], []
    for c in range(PAIR):
        source = place_ref[3 + chunk * (PAIR // 2) + c // 2]
        low = jnp.where(source == 0, data0_ref[c % 2, 0], data1_ref[c % 2, 0])
        high = jnp.where(source == 2, data2_ref[c % 2, 0], data3_ref[c % 2, 0])
        measured = jnp.where(source < 2, low, high).astype(F32)
        s = spectra[:, c * 256 : (c + 1) * 256] - measured
        res_re, res_im = mask * s[:, :NX], mask * s[:, NX:]
        tops += [res_re, res_im]
        bottoms += [-res_im, res_re]
    stacked = jnp.concatenate([jnp.concatenate(tops, axis=1), jnp.concatenate(bottoms, axis=1)], axis=0).astype(BF16)
    columns = matmul(table, stacked).astype(BF16)
    rows = jnp.concatenate([columns[:, c * 256 : (c + 1) * 256] for c in range(PAIR)], axis=0)
    rows = matmul(rows, back_table)
    real = imag = 0.0
    for c in range(PAIR):
        b = rows[c * NY : (c + 1) * NY]
        back_re, back_im = b[:, :NX], b[:, NX:]
        real += sens_re[c] * back_re + sens_im[c] * back_im
        imag += sens_re[c] * back_im - sens_im[c] * back_re
    both = jnp.concatenate([real, imag], axis=1)
    total = jnp.where(chunk == 0, both, acc_ref[...] + both)
    acc_ref[...] = total
    out_ref[...] = total.astype(BF16).reshape(out_ref.shape)


def pick_kernel(place_ref, sens_ref, out_ref):
    to, frm = iota((64, 128), 0), iota((64, 128), 1)
    turn = as_matrix((to & 15) * Z + (to >> 4) * 2 + place_ref[1] == frm)
    for g in range(16 // SHARE):
        for c in range(2):
            picked = matmul(turn, sens_ref[g, 0, c]).astype(BF16)
            out_ref[g * SHARE : (g + 1) * SHARE, c] = picked.reshape(SHARE, 16, 256)


def turn_kernel(place_ref, data_ref, *out_refs):
    to, frm = iota((128, 128), 0), iota((128, 128), 1)
    depth = (((to >> 5) ^ place_ref[2]) << 1) + (((to >> 4) & 1) ^ place_ref[1])
    turn = as_matrix((to & 15) * Z + depth == frm)
    for b in range(data_ref.shape[1]):
        turned = matmul(turn, data_ref[0, b]).astype(BF16).reshape(SHARE, 2, 16, 256)
        for j in range(SHARE):
            out_refs[j][0, :, b * 16 : (b + 1) * 16] = turned[j]


def full(shape):
    return pl.BlockSpec(shape, lambda *_: (0,) * len(shape))


def call(kernel, place, arrays, grid, in_specs, out_specs, out_shape, scratch, name, micros, vmem):
    return pl.pallas_call(
        kernel,
        grid_spec=pltpu.PrefetchScalarGridSpec(
            num_scalar_prefetch=1, grid=grid, in_specs=in_specs, out_specs=out_specs, scratch_shapes=scratch
        ),
        out_shape=out_shape,
        compiler_params=pltpu.CompilerParams(vmem_limit_bytes=vmem * 2**20),
        cost_estimate=pl.CostEstimate(flops=0, bytes_accessed=int(micros * 3e6), transcendentals=0),
        name=name,
    )(place, *arrays)


def weight_slots():
    return pltpu.VMEM((256 // STEP, STEP, 64, 128), BF16), pltpu.SemaphoreType.DMA((256 // STEP,))


def warp_forward(place, columns, weights, prior, current):
    shape = (16, 128 // SHARE, 256)
    return call(
        warp_kernel,
        place,
        (columns, weights, prior, current),
        (256 // STEP,),
        [
            pl.BlockSpec((8 * STEP, 1), lambda i, p: (i, 0)),
            pl.BlockSpec(memory_space=pltpu.HBM),
            full((128, 256)),
            full((128, 256)),
        ],
        full(shape),
        jax.ShapeDtypeStruct(shape, BF16),
        [pltpu.VMEM((128, 256), F32), *weight_slots()],
        "warp_forward",
        8,
        32,
    )


def warp_adjoint(place, columns, rows, weights, parts):
    return call(
        adjoint_kernel,
        place,
        (columns, rows, weights, parts),
        (256 // STEP,),
        [
            pl.BlockSpec((8 * STEP, 1), lambda i, p: (i, 0)),
            pl.BlockSpec((1, 8 * STEP), lambda i, p: (0, i)),
            pl.BlockSpec(memory_space=pltpu.HBM),
            full((16, 128 // SHARE, 256)),
        ],
        [full((128, 256)), full((128, 256))],
        [jax.ShapeDtypeStruct((128, 256), F32), jax.ShapeDtypeStruct((128, 256), BF16)],
        [pltpu.VMEM((128, 256), BF16), pltpu.VMEM((128, 256), F32), *weight_slots()],
        "warp_adjoint",
        8,
        32,
    )


def data_gradient(place, moved, own, other, measured, mask):
    matrix = row_matrix()
    return call(
        data_kernel,
        place,
        (moved, *own, *other, *measured, mask, jnp.asarray(np.concatenate([matrix, matrix.T, column_table()], axis=1))),
        (2, 8 // PAIR),
        [
            pl.BlockSpec((16, 1, 16, 256), lambda z, c, p: (0, z, 0, 0)),
            *[full((16, 2, 16, 256))] * 8,
            *[pl.BlockSpec((2, 1, NY, 256), lambda z, c, p: (0, z, 0, 0))] * 4,
            full((NY, NX)),
            full((256, 1024)),
        ],
        pl.BlockSpec((16, 1, 16, 256), lambda z, c, p: (0, z, 0, 0)),
        jax.ShapeDtypeStruct((16, 2, 16, 256), BF16),
        [pltpu.VMEM((NY, 256), F32)],
        "data_gradient",
        8,
        40,
    )


def pick_share(place, sensitivity):
    return call(
        pick_kernel,
        place,
        (sensitivity.reshape(4, 4, 2, 128, 256),),
        (1,),
        [pl.BlockSpec((4, 1, 2, 128, 256), lambda g, p: (0, p[0], 0, 0, 0))],
        full((16, 2, 16, 256)),
        jax.ShapeDtypeStruct((16, 2, 16, 256), BF16),
        [],
        "pick_share",
        1,
        60,
    )


def turn_data(place, data):
    blocks = 8
    return call(
        turn_kernel,
        place,
        (data.reshape(2, 16, 128, 256),),
        (2, 16 // blocks),
        [pl.BlockSpec((1, blocks, 128, 256), lambda c, b, p: (c, b, 0, 0))],
        [pl.BlockSpec((1, 2, 16 * blocks, 256), lambda c, b, p: (c, 0, b, 0))] * SHARE,
        [jax.ShapeDtypeStruct((2, 2, NY, 256), BF16)] * SHARE,
        [],
        "turn_data",
        3,
        60,
    )


def on_device(cine_image, warp_blocks, warp_index, sample_mask, kspace_data, sensitivity):
    loop_axes, coil = ("y", "half", "core"), ("group", "member")
    row, core, member = lax.axis_index("y"), lax.axis_index("core"), lax.axis_index("member")
    offsets = (0, 1, -1, 2)
    place = jnp.stack([row, core, member, *[((row + d) % 4) ^ member for d in offsets]])
    forward = [(i, (i + 1) % 16) for i in range(16)]
    backward = [((i + 1) % 16, i) for i in range(16)]
    current = cine_image.reshape(128, 256)
    prior = lax.ppermute(current, loop_axes, forward)

    sens, prior, kspace_data = lax.optimization_barrier((pick_share(place, sensitivity), prior, kspace_data))
    sens = lax.all_to_all(sens, coil, 0, 0, tiled=True)
    measured = turn_data(place, kspace_data)
    measured = [
        piece if j == 0 else lax.ppermute(piece, "member", [(i, i ^ j) for i in range(SHARE)])
        for j, piece in enumerate(measured)
    ]

    weights = warp_blocks.reshape(256, 2, 32, 128).transpose(0, 2, 1, 3).reshape(256, 64, 128)
    weights = pltpu.with_memory_space_constraint(weights, pltpu.HBM)
    index = warp_index[0] - lax.axis_index(coil) * 256
    index = jnp.broadcast_to(index[:, :, None], (256, 2, 4)).reshape(2048)
    columns, rows = index.reshape(2048, 1), index.reshape(1, 2048)
    prior, sens, measured[0], columns = lax.optimization_barrier((prior, sens, measured[0], columns))
    moved = warp_forward(place, columns, weights, prior, current)
    up, down = [(i, (i + 1) % 4) for i in range(4)], [(i, (i - 1) % 4) for i in range(4)]
    shared = [lax.ppermute(sens, "y", down), lax.ppermute(sens, "y", up)]
    shared.append(lax.ppermute(shared[0], "y", down))
    moved = lax.all_to_all(moved, coil, 0, 0, tiled=True).reshape(16, 2, 16, 256)
    sens = [sens, *shared]
    other = [lax.ppermute(piece, "core", [(0, 1), (1, 0)]) for piece in sens]
    moved, sens, other, measured = lax.optimization_barrier((moved, sens, other, measured))
    parts = data_gradient(place, moved, sens, other, measured, sample_mask[0])
    parts = lax.all_to_all(parts, coil, 0, 0, tiled=True).reshape(16, 32, 256)
    grad, pulled = warp_adjoint(place, columns, rows, weights, parts)
    from_next = lax.ppermute(pulled, loop_axes, backward)
    return (grad + from_next.astype(F32)).reshape(1, 16, Z, 256)


def solution(mesh):
    inner = Mesh(mesh.devices.reshape(4, 2, 2, 16 // SHARE, SHARE), ("y", "half", "core", "group", "member"))
    bins, coil = ("y", "half", "core"), ("group", "member")
    return jax.shard_map(
        on_device,
        mesh=inner,
        in_specs=(
            P(bins, coil, None, None),
            P(bins, coil, None, None),
            P(bins, coil, None),
            P(bins, None, None),
            P(bins, coil, None, None, None),
            P(None, coil, None, None),
        ),
        out_specs=P(bins, coil, None, None),
        check_vma=False,
    )
```

```python
import jax
import jax.numpy as jnp
import numpy as np
from jax import lax
from jax.experimental import pallas as pl
from jax.experimental.pallas import tpu as pltpu
from jax.sharding import Mesh
from jax.sharding import PartitionSpec as P

NY = 256
NX = 128
Z = 8
SHARE = 4
PAIR = 8
STEP = 128

F32 = jnp.float32
BF16 = jnp.bfloat16


def cosine_sine(length):
    positions = np.arange(length)
    phases = positions[:, None] * positions[None, :] % length
    angles = phases * (2.0 * np.pi / length)
    return np.cos(angles) / np.sqrt(length), np.sin(angles) / np.sqrt(length)


def row_matrix():
    cosine, sine = cosine_sine(NX)
    return np.block([[cosine, -sine], [sine, cosine]]).astype(BF16)


def column_table():
    return np.concatenate(cosine_sine(NY), axis=1).astype(BF16)


def iota(shape, axis):
    return lax.broadcasted_iota(jnp.int32, shape, axis)


def matmul(a, b):
    return jnp.dot(a, b, preferred_element_type=F32)


def high_low(values):
    high = values.astype(BF16)
    return high, (values - high.astype(F32)).astype(BF16)


def sublane_roles(rows):
    r = iota((rows, 128), 0)
    return r, (r >> 2) & 1, (r >> 1) & 1, r & 1


def shift_lanes(values, distance):
    return jnp.where(
        distance == 1,
        pltpu.roll(values, 1, 1),
        jnp.where(distance == -1, pltpu.roll(values, 127, 1), values),
    )


def as_matrix(condition):
    return condition.astype(F32).astype(BF16)


def depth_major(core):
    to, frm = iota((128, 128), 0), iota((128, 128), 1)
    return as_matrix((to & 15) * Z + ((to >> 4) ^ core) == frm)


def fetches(w_ref, slot_ref, sems):
    return [
        pltpu.make_async_copy(w_ref.at[pl.ds(i * STEP, STEP)], slot_ref.at[i], sems.at[i]) for i in range(256 // STEP)
    ]


def wait_for(step, copies):
    for i, copy in enumerate(copies):
        pl.when(step == i)(copy.wait)


def warp_kernel(place_ref, col_ref, w_ref, prior_ref, cur_ref, out_ref, acc_ref, slot_ref, sems):
    step = pl.program_id(0)
    copies = fetches(w_ref, slot_ref, sems)

    @pl.when(step == 0)
    def _():
        for copy in copies:
            copy.start()

    rows = 8 * STEP
    index = col_ref[...]
    r, slot, odd, imag = sublane_roles(rows)
    lane = iota((rows, 128), 1)
    half = lane >> 6
    chosen = (lane == (index >> 1)).astype(F32).astype(BF16)
    both = matmul(chosen, prior_ref[...])
    v = jnp.where(imag == 1, both[:, 128:], both[:, :128])
    v = jnp.where((index & 1) == odd, v, pltpu.roll(v, 64, 1))
    v = jnp.where(half == odd, v, 0.0)
    wait_for(step, copies)
    f = lax.dot_general(
        v.reshape(STEP // 4, 32, 128).astype(BF16),
        slot_ref[step].reshape(STEP // 4, 256, 128),
        (((2,), (2,)), ((0,), (0,))),
        preferred_element_type=F32,
    ).reshape(rows, 256)
    f = jnp.where(((r >> 4) & 1) == 0, f[:, :128], f[:, 128:])
    f = jnp.where(((lane & 1) == slot) & (half == ((r >> 3) & 1)), f, 0.0)
    f = shift_lanes(f, odd - slot)
    f = jnp.concatenate([jnp.where(imag == 0, f, 0.0), jnp.where(imag == 1, f, 0.0)], axis=1)
    lines = STEP // 2
    gather = as_matrix(iota((lines, rows), 1) >> 4 == iota((lines, rows), 0))
    high, low = high_low(f)
    acc_ref[pl.ds(pl.multiple_of(step * lines, lines), lines), :] = matmul(gather, high) + matmul(gather, low)

    @pl.when(step == pl.num_programs(0) - 1)
    def _():
        moved = (cur_ref[...].astype(F32) + acc_ref[...]).astype(BF16)
        turned = matmul(depth_major(place_ref[1]), moved).astype(BF16).reshape(SHARE, 128 // SHARE, 256)
        for g in range(16 // SHARE):
            out_ref[g * SHARE : (g + 1) * SHARE] = turned


def adjoint_kernel(place_ref, col_ref, row_ref, w_ref, parts_ref, grad_ref, pulled_ref, image_ref, acc_ref, slot_ref, sems):
    step = pl.program_id(0)
    copies = fetches(w_ref, slot_ref, sems)
    rows = 8 * STEP

    @pl.when(step == 0)
    def _():
        for copy in copies:
            copy.start()
        total = parts_ref[0:SHARE].astype(F32)
        for g in range(1, 16 // SHARE):
            total = total + parts_ref[g * SHARE : (g + 1) * SHARE].astype(F32)
        total = total.reshape(128, 256)
        frm, to = iota((128, 128), 1), iota((128, 128), 0)
        turn = as_matrix((frm & 15) * Z + ((frm >> 4) ^ place_ref[1]) == to)
        high, low = high_low(total)
        lowest = (total - high.astype(F32) - low.astype(F32)).astype(BF16)
        grad = matmul(turn, high) + matmul(turn, low) + matmul(turn, lowest)
        grad_ref[...] = grad
        image_ref[...] = grad.astype(BF16)
        acc_ref[...] = jnp.zeros_like(acc_ref)

    index = col_ref[...]
    r, slot, odd, imag = sublane_roles(rows)
    lane = iota((rows, 128), 1)
    half = lane >> 6
    chosen = (lane == step * (STEP // 2) + (r >> 4)).astype(F32).astype(BF16)
    both = matmul(chosen, image_ref[...])
    v = jnp.where(imag == 1, both[:, 128:], both[:, :128])
    v = jnp.where(half == ((r >> 3) & 1), v, pltpu.roll(v, 64, 1))
    v = jnp.where((lane & 1) == odd, v, 0.0)
    v = shift_lanes(v, slot - odd)
    place4 = (r >> 3) & 3
    v = jnp.concatenate([jnp.where(half == place4, v, 0.0), jnp.where(half + 2 == place4, v, 0.0)], axis=1)
    wait_for(step, copies)
    f = lax.dot_general(
        v.reshape(STEP // 4, 32, 256).astype(BF16),
        slot_ref[step].reshape(STEP // 4, 256, 128),
        (((2,), (1,)), ((0,), (0,))),
        preferred_element_type=F32,
    ).reshape(rows, 128)
    f = jnp.where(half == odd, f, 0.0)
    f = f + pltpu.roll(f, 64, 1)
    f = jnp.where(half == (index & 1), f, 0.0)
    f = jnp.concatenate([jnp.where(imag == 0, f, 0.0), jnp.where(imag == 1, f, 0.0)], axis=1)
    scatter = (iota((128, rows), 0) == (row_ref[...] >> 1)).astype(F32).astype(BF16)
    high, low = high_low(f)
    acc_ref[...] += matmul(scatter, high) + matmul(scatter, low)

    @pl.when(step == pl.num_programs(0) - 1)
    def _():
        pulled_ref[...] = acc_ref[...].astype(BF16)


def data_kernel(
    place_ref,
    moved_ref,
    own0_ref,
    own1_ref,
    own2_ref,
    own3_ref,
    other0_ref,
    other1_ref,
    other2_ref,
    other3_ref,
    data0_ref,
    data1_ref,
    data2_ref,
    data3_ref,
    mask_ref,
    tables_ref,
    out_ref,
    acc_ref,
):
    own_refs = (own0_ref, own1_ref, own2_ref, own3_ref)
    other_refs = (other0_ref, other1_ref, other2_ref, other3_ref)
    depth, chunk = pl.program_id(0), pl.program_id(1)
    moved = moved_ref[...].reshape(NY, 256).astype(F32)
    image_re, image_im = moved[:, :NX], moved[:, NX:]
    mask = mask_ref[...].astype(F32)
    row_table, back_table, table = tables_ref[:, :256], tables_ref[:, 256:512], tables_ref[:, 512:]
    sens_re, sens_im, images = [], [], []
    for c in range(PAIR):
        sens = jnp.where(depth == 0, own_refs[c // 2][:, c % 2], other_refs[c // 2][:, c % 2])
        sens = sens.reshape(NY, 256).astype(F32)
        sens_re.append(sens[:, :NX])
        sens_im.append(sens[:, NX:])
        re = sens_re[c] * image_re - sens_im[c] * image_im
        im = sens_re[c] * image_im + sens_im[c] * image_re
        images.append(jnp.concatenate([re, im], axis=1).astype(BF16))
    spectra = matmul(jnp.concatenate(images, axis=0), row_table)
    tops, bottoms = [], []
    for c in range(PAIR):
        s = spectra[c * NY : (c + 1) * NY]
        tops.append(s)
        bottoms += [s[:, NX:], -s[:, :NX]]
    stacked = jnp.concatenate([jnp.concatenate(tops, axis=1), jnp.concatenate(bottoms, axis=1)], axis=0).astype(BF16)
    spectra = matmul(table, stacked)
    tops, bottoms = [], []
    for c in range(PAIR):
        source = place_ref[3 + chunk * (PAIR // 2) + c // 2]
        low = jnp.where(source == 0, data0_ref[c % 2, 0], data1_ref[c % 2, 0])
        high = jnp.where(source == 2, data2_ref[c % 2, 0], data3_ref[c % 2, 0])
        measured = jnp.where(source < 2, low, high).astype(F32)
        s = spectra[:, c * 256 : (c + 1) * 256] - measured
        res_re, res_im = mask * s[:, :NX], mask * s[:, NX:]
        tops += [res_re, res_im]
        bottoms += [-res_im, res_re]
    stacked = jnp.concatenate([jnp.concatenate(tops, axis=1), jnp.concatenate(bottoms, axis=1)], axis=0).astype(BF16)
    columns = matmul(table, stacked).astype(BF16)
    rows = jnp.concatenate([columns[:, c * 256 : (c + 1) * 256] for c in range(PAIR)], axis=0)
    rows = matmul(rows, back_table)
    real = imag = 0.0
    for c in range(PAIR):
        b = rows[c * NY : (c + 1) * NY]
        back_re, back_im = b[:, :NX], b[:, NX:]
        real += sens_re[c] * back_re + sens_im[c] * back_im
        imag += sens_re[c] * back_im - sens_im[c] * back_re
    both = jnp.concatenate([real, imag], axis=1)
    total = jnp.where(chunk == 0, both, acc_ref[...] + both)
    acc_ref[...] = total
    out_ref[...] = total.astype(BF16).reshape(out_ref.shape)


def pick_kernel(place_ref, sens_ref, out_ref):
    to, frm = iota((64, 128), 0), iota((64, 128), 1)
    turn = as_matrix((to & 15) * Z + (to >> 4) * 2 + (place_ref[0] & 1) == frm)
    for g in range(16 // SHARE):
        for c in range(2):
            picked = matmul(turn, sens_ref[g, 0, c]).astype(BF16)
            out_ref[g * SHARE : (g + 1) * SHARE, c] = picked.reshape(SHARE, 16, 256)


def turn_kernel(place_ref, data_ref, *out_refs):
    to, frm = iota((128, 128), 0), iota((128, 128), 1)
    depth = (((to >> 5) ^ place_ref[2]) << 1) + (((to >> 4) & 1) ^ place_ref[1])
    turn = as_matrix((to & 15) * Z + depth == frm)
    for b in range(data_ref.shape[1]):
        turned = matmul(turn, data_ref[0, b]).astype(BF16).reshape(SHARE, 2, 16, 256)
        for j in range(SHARE):
            out_refs[j][0, :, b * 16 : (b + 1) * 16] = turned[j]


def full(shape):
    return pl.BlockSpec(shape, lambda *_: (0,) * len(shape))


def call(kernel, place, arrays, grid, in_specs, out_specs, out_shape, scratch, name, micros, vmem):
    return pl.pallas_call(
        kernel,
        grid_spec=pltpu.PrefetchScalarGridSpec(
            num_scalar_prefetch=1, grid=grid, in_specs=in_specs, out_specs=out_specs, scratch_shapes=scratch
        ),
        out_shape=out_shape,
        compiler_params=pltpu.CompilerParams(vmem_limit_bytes=vmem * 2**20),
        cost_estimate=pl.CostEstimate(flops=0, bytes_accessed=int(micros * 3e6), transcendentals=0),
        name=name,
    )(place, *arrays)


def weight_slots():
    return pltpu.VMEM((256 // STEP, STEP, 64, 128), BF16), pltpu.SemaphoreType.DMA((256 // STEP,))


def warp_forward(place, columns, weights, prior, current):
    shape = (16, 128 // SHARE, 256)
    return call(
        warp_kernel,
        place,
        (columns, weights, prior, current),
        (256 // STEP,),
        [
            pl.BlockSpec((8 * STEP, 1), lambda i, p: (i, 0)),
            pl.BlockSpec(memory_space=pltpu.HBM),
            full((128, 256)),
            full((128, 256)),
        ],
        full(shape),
        jax.ShapeDtypeStruct(shape, BF16),
        [pltpu.VMEM((128, 256), F32), *weight_slots()],
        "warp_forward",
        8,
        32,
    )


def warp_adjoint(place, columns, rows, weights, parts):
    return call(
        adjoint_kernel,
        place,
        (columns, rows, weights, parts),
        (256 // STEP,),
        [
            pl.BlockSpec((8 * STEP, 1), lambda i, p: (i, 0)),
            pl.BlockSpec((1, 8 * STEP), lambda i, p: (0, i)),
            pl.BlockSpec(memory_space=pltpu.HBM),
            full((16, 128 // SHARE, 256)),
        ],
        [full((128, 256)), full((128, 256))],
        [jax.ShapeDtypeStruct((128, 256), F32), jax.ShapeDtypeStruct((128, 256), BF16)],
        [pltpu.VMEM((128, 256), BF16), pltpu.VMEM((128, 256), F32), *weight_slots()],
        "warp_adjoint",
        8,
        32,
    )


def data_gradient(place, moved, own, other, measured, mask):
    matrix = row_matrix()
    return call(
        data_kernel,
        place,
        (moved, *own, *other, *measured, mask, jnp.asarray(np.concatenate([matrix, matrix.T, column_table()], axis=1))),
        (2, 8 // PAIR),
        [
            pl.BlockSpec((16, 1, 16, 256), lambda z, c, p: (0, z, 0, 0)),
            *[full((16, 2, 16, 256))] * 8,
            *[pl.BlockSpec((2, 1, NY, 256), lambda z, c, p: (0, z, 0, 0))] * 4,
            full((NY, NX)),
            full((256, 1024)),
        ],
        pl.BlockSpec((16, 1, 16, 256), lambda z, c, p: (0, z, 0, 0)),
        jax.ShapeDtypeStruct((16, 2, 16, 256), BF16),
        [pltpu.VMEM((NY, 256), F32)],
        "data_gradient",
        8,
        40,
    )


def pick_share(place, sensitivity):
    return call(
        pick_kernel,
        place,
        (sensitivity.reshape(4, 4, 2, 128, 256),),
        (1,),
        [pl.BlockSpec((4, 1, 2, 128, 256), lambda g, p: (0, p[0] >> 1, 0, 0, 0))],
        full((16, 2, 16, 256)),
        jax.ShapeDtypeStruct((16, 2, 16, 256), BF16),
        [],
        "pick_share",
        1,
        60,
    )


def turn_data(place, data):
    blocks = 16
    return call(
        turn_kernel,
        place,
        (data.reshape(2, 16, 128, 256),),
        (2, 16 // blocks),
        [pl.BlockSpec((1, blocks, 128, 256), lambda c, b, p: (c, b, 0, 0))],
        [pl.BlockSpec((1, 2, 16 * blocks, 256), lambda c, b, p: (c, 0, b, 0))] * SHARE,
        [jax.ShapeDtypeStruct((2, 2, NY, 256), BF16)] * SHARE,
        [],
        "turn_data",
        3,
        60,
    )


def on_device(cine_image, warp_blocks, warp_index, sample_mask, kspace_data, sensitivity):
    loop_axes, coil = ("y", "half", "core"), ("group", "member")
    row, core, member = lax.axis_index("y"), lax.axis_index("core"), lax.axis_index("member")
    offsets = (0, 1, -1, 2)
    place = jnp.stack([row, core, member, *[((row + d) % 4) ^ member for d in offsets]])
    forward = [(i, (i + 1) % 16) for i in range(16)]
    backward = [((i + 1) % 16, i) for i in range(16)]
    current = cine_image.reshape(128, 256)
    prior = lax.ppermute(current, loop_axes, forward)

    sens, prior, kspace_data = lax.optimization_barrier((pick_share((row * 2 + core).reshape(1), sensitivity), prior, kspace_data))
    sens = lax.all_to_all(sens, coil, 0, 0, tiled=True)
    measured = turn_data(place, kspace_data)
    measured = [
        piece if j == 0 else lax.ppermute(piece, "member", [(i, i ^ j) for i in range(SHARE)])
        for j, piece in enumerate(measured)
    ]

    weights = warp_blocks.reshape(256, 2, 32, 128).transpose(0, 2, 1, 3).reshape(256, 64, 128)
    weights = pltpu.with_memory_space_constraint(weights, pltpu.HBM)
    index = warp_index[0] - lax.axis_index(coil) * 256
    index = jnp.broadcast_to(index[:, :, None], (256, 2, 4)).reshape(2048)
    columns, rows = index.reshape(2048, 1), index.reshape(1, 2048)
    prior, sens, measured[0], columns = lax.optimization_barrier((prior, sens, measured[0], columns))
    moved = warp_forward(place, columns, weights, prior, current)
    up, down = [(i, (i + 1) % 4) for i in range(4)], [(i, (i - 1) % 4) for i in range(4)]
    shared = [lax.ppermute(sens, "y", down), lax.ppermute(sens, "y", up)]
    shared.append(lax.ppermute(shared[0], "y", down))
    moved = lax.all_to_all(moved, coil, 0, 0, tiled=True).reshape(16, 2, 16, 256)
    sens = [sens, *shared]
    other = [lax.ppermute(piece, "core", [(0, 1), (1, 0)]) for piece in sens]
    moved, sens, other, measured = lax.optimization_barrier((moved, sens, other, measured))
    other = [pltpu.with_memory_space_constraint(piece, pltpu.HBM) for piece in other]
    parts = data_gradient(place, moved, sens, other, measured, sample_mask[0])
    parts = lax.all_to_all(parts, coil, 0, 0, tiled=True).reshape(16, 32, 256)
    grad, pulled = warp_adjoint(place, columns, rows, weights, parts)
    from_next = lax.ppermute(pulled, loop_axes, backward)
    return (grad + from_next.astype(F32)).reshape(1, 16, Z, 256)


def solution(mesh):
    inner = Mesh(mesh.devices.reshape(4, 2, 2, 16 // SHARE, SHARE), ("y", "half", "core", "group", "member"))
    bins, coil = ("y", "half", "core"), ("group", "member")
    return jax.shard_map(
        on_device,
        mesh=inner,
        in_specs=(
            P(bins, coil, None, None),
            P(bins, coil, None, None),
            P(bins, coil, None),
            P(bins, None, None),
            P(bins, coil, None, None, None),
            P(None, coil, None, None),
        ),
        out_specs=P(bins, coil, None, None),
        check_vma=False,
    )
```

```python
import jax
import jax.numpy as jnp
import numpy as np
from jax import lax
from jax.experimental import pallas as pl
from jax.experimental.pallas import tpu as pltpu
from jax.sharding import Mesh
from jax.sharding import PartitionSpec as P

NY = 256
NX = 128
Z = 8
SHARE = 4
PAIR = 8
STEP = 128

F32 = jnp.float32
BF16 = jnp.bfloat16


def cosine_sine(length):
    positions = np.arange(length)
    phases = positions[:, None] * positions[None, :] % length
    angles = phases * (2.0 * np.pi / length)
    return np.cos(angles) / np.sqrt(length), np.sin(angles) / np.sqrt(length)


def row_matrix():
    cosine, sine = cosine_sine(NX)
    return np.block([[cosine, -sine], [sine, cosine]]).astype(BF16)


def column_table():
    return np.concatenate(cosine_sine(NY), axis=1).astype(BF16)


def iota(shape, axis):
    return lax.broadcasted_iota(jnp.int32, shape, axis)


def matmul(a, b):
    return jnp.dot(a, b, preferred_element_type=F32)


def high_low(values):
    high = values.astype(BF16)
    return high, (values - high.astype(F32)).astype(BF16)


def sublane_roles(rows):
    r = iota((rows, 128), 0)
    return r, (r >> 2) & 1, (r >> 1) & 1, r & 1


def shift_lanes(values, distance):
    return jnp.where(
        distance == 1,
        pltpu.roll(values, 1, 1),
        jnp.where(distance == -1, pltpu.roll(values, 127, 1), values),
    )


def as_matrix(condition):
    return condition.astype(F32).astype(BF16)


def depth_major(core):
    to, frm = iota((128, 128), 0), iota((128, 128), 1)
    return as_matrix((to & 15) * Z + ((to >> 4) ^ core) == frm)


def fetches(w_ref, slot_ref, sems):
    return [
        pltpu.make_async_copy(w_ref.at[pl.ds(i * STEP, STEP)], slot_ref.at[i], sems.at[i]) for i in range(256 // STEP)
    ]


def wait_for(step, copies):
    for i, copy in enumerate(copies):
        pl.when(step == i)(copy.wait)


def warp_kernel(place_ref, col_ref, w_ref, prior_ref, cur_ref, out_ref, acc_ref, slot_ref, sems):
    step = pl.program_id(0)
    copies = fetches(w_ref, slot_ref, sems)

    @pl.when(step == 0)
    def _():
        for copy in copies:
            copy.start()

    rows = 8 * STEP
    index = col_ref[...]
    r, slot, odd, imag = sublane_roles(rows)
    lane = iota((rows, 128), 1)
    half = lane >> 6
    chosen = (lane == (index >> 1)).astype(F32).astype(BF16)
    both = matmul(chosen, prior_ref[...])
    v = jnp.where(imag == 1, both[:, 128:], both[:, :128])
    v = jnp.where((index & 1) == odd, v, pltpu.roll(v, 64, 1))
    v = jnp.where(half == odd, v, 0.0)
    wait_for(step, copies)
    f = lax.dot_general(
        v.reshape(STEP // 4, 32, 128).astype(BF16),
        slot_ref[step].reshape(STEP // 4, 256, 128),
        (((2,), (2,)), ((0,), (0,))),
        preferred_element_type=F32,
    ).reshape(rows, 256)
    f = jnp.where(((r >> 4) & 1) == 0, f[:, :128], f[:, 128:])
    f = jnp.where(((lane & 1) == slot) & (half == ((r >> 3) & 1)), f, 0.0)
    f = shift_lanes(f, odd - slot)
    f = jnp.concatenate([jnp.where(imag == 0, f, 0.0), jnp.where(imag == 1, f, 0.0)], axis=1)
    lines = STEP // 2
    gather = as_matrix(iota((lines, rows), 1) >> 4 == iota((lines, rows), 0))
    high, low = high_low(f)
    acc_ref[pl.ds(pl.multiple_of(step * lines, lines), lines), :] = matmul(gather, high) + matmul(gather, low)

    @pl.when(step == pl.num_programs(0) - 1)
    def _():
        moved = (cur_ref[...].astype(F32) + acc_ref[...]).astype(BF16)
        turned = matmul(depth_major(place_ref[1]), moved).astype(BF16).reshape(SHARE, 128 // SHARE, 256)
        for g in range(16 // SHARE):
            out_ref[g * SHARE : (g + 1) * SHARE] = turned


def adjoint_kernel(place_ref, col_ref, row_ref, w_ref, parts_ref, grad_ref, pulled_ref, image_ref, acc_ref, slot_ref, sems):
    step = pl.program_id(0)
    copies = fetches(w_ref, slot_ref, sems)
    rows = 8 * STEP

    @pl.when(step == 0)
    def _():
        for copy in copies:
            copy.start()
        total = parts_ref[0:SHARE].astype(F32)
        for g in range(1, 16 // SHARE):
            total = total + parts_ref[g * SHARE : (g + 1) * SHARE].astype(F32)
        total = total.reshape(128, 256)
        frm, to = iota((128, 128), 1), iota((128, 128), 0)
        turn = as_matrix((frm & 15) * Z + ((frm >> 4) ^ place_ref[1]) == to)
        high, low = high_low(total)
        lowest = (total - high.astype(F32) - low.astype(F32)).astype(BF16)
        grad = matmul(turn, high) + matmul(turn, low) + matmul(turn, lowest)
        grad_ref[...] = grad
        image_ref[...] = grad.astype(BF16)
        acc_ref[...] = jnp.zeros_like(acc_ref)

    index = col_ref[...]
    r, slot, odd, imag = sublane_roles(rows)
    lane = iota((rows, 128), 1)
    half = lane >> 6
    chosen = (lane == step * (STEP // 2) + (r >> 4)).astype(F32).astype(BF16)
    both = matmul(chosen, image_ref[...])
    v = jnp.where(imag == 1, both[:, 128:], both[:, :128])
    v = jnp.where(half == ((r >> 3) & 1), v, pltpu.roll(v, 64, 1))
    v = jnp.where((lane & 1) == odd, v, 0.0)
    v = shift_lanes(v, slot - odd)
    place4 = (r >> 3) & 3
    v = jnp.concatenate([jnp.where(half == place4, v, 0.0), jnp.where(half + 2 == place4, v, 0.0)], axis=1)
    wait_for(step, copies)
    f = lax.dot_general(
        v.reshape(STEP // 4, 32, 256).astype(BF16),
        slot_ref[step].reshape(STEP // 4, 256, 128),
        (((2,), (1,)), ((0,), (0,))),
        preferred_element_type=F32,
    ).reshape(rows, 128)
    f = jnp.where(half == odd, f, 0.0)
    f = f + pltpu.roll(f, 64, 1)
    f = jnp.where(half == (index & 1), f, 0.0)
    f = jnp.concatenate([jnp.where(imag == 0, f, 0.0), jnp.where(imag == 1, f, 0.0)], axis=1)
    scatter = (iota((128, rows), 0) == (row_ref[...] >> 1)).astype(F32).astype(BF16)
    high, low = high_low(f)
    acc_ref[...] += matmul(scatter, high) + matmul(scatter, low)

    @pl.when(step == pl.num_programs(0) - 1)
    def _():
        pulled_ref[...] = acc_ref[...].astype(BF16)


def data_kernel(
    place_ref,
    moved_ref,
    own0_ref,
    own1_ref,
    own2_ref,
    own3_ref,
    other0_ref,
    other1_ref,
    other2_ref,
    other3_ref,
    data0_ref,
    data1_ref,
    data2_ref,
    data3_ref,
    mask_ref,
    tables_ref,
    out_ref,
    acc_ref,
):
    own_refs = (own0_ref, own1_ref, own2_ref, own3_ref)
    other_refs = (other0_ref, other1_ref, other2_ref, other3_ref)
    depth, chunk = pl.program_id(0), pl.program_id(1)
    moved = moved_ref[...].reshape(NY, 256).astype(F32)
    image_re, image_im = moved[:, :NX], moved[:, NX:]
    mask = mask_ref[...].astype(F32)
    row_table, back_table, table = tables_ref[:, :256], tables_ref[:, 256:512], tables_ref[:, 512:]
    sens_re, sens_im, images = [], [], []
    for c in range(PAIR):
        sens = jnp.where(depth == 0, own_refs[c // 2][:, c % 2], other_refs[c // 2][:, c % 2])
        sens = sens.reshape(NY, 256).astype(F32)
        sens_re.append(sens[:, :NX])
        sens_im.append(sens[:, NX:])
        re = sens_re[c] * image_re - sens_im[c] * image_im
        im = sens_re[c] * image_im + sens_im[c] * image_re
        images.append(jnp.concatenate([re, im], axis=1).astype(BF16))
    spectra = matmul(jnp.concatenate(images, axis=0), row_table)
    tops, bottoms = [], []
    for c in range(PAIR):
        s = spectra[c * NY : (c + 1) * NY]
        tops.append(s)
        bottoms += [s[:, NX:], -s[:, :NX]]
    stacked = jnp.concatenate([jnp.concatenate(tops, axis=1), jnp.concatenate(bottoms, axis=1)], axis=0).astype(BF16)
    spectra = matmul(table, stacked)
    tops, bottoms = [], []
    for c in range(PAIR):
        source = place_ref[3 + chunk * (PAIR // 2) + c // 2]
        low = jnp.where(source == 0, data0_ref[c % 2, 0], data1_ref[c % 2, 0])
        high = jnp.where(source == 2, data2_ref[c % 2, 0], data3_ref[c % 2, 0])
        measured = jnp.where(source < 2, low, high).astype(F32)
        s = spectra[:, c * 256 : (c + 1) * 256] - measured
        res_re, res_im = mask * s[:, :NX], mask * s[:, NX:]
        tops += [res_re, res_im]
        bottoms += [-res_im, res_re]
    stacked = jnp.concatenate([jnp.concatenate(tops, axis=1), jnp.concatenate(bottoms, axis=1)], axis=0).astype(BF16)
    columns = matmul(table, stacked).astype(BF16)
    rows = jnp.concatenate([columns[:, c * 256 : (c + 1) * 256] for c in range(PAIR)], axis=0)
    rows = matmul(rows, back_table)
    real = imag = 0.0
    for c in range(PAIR):
        b = rows[c * NY : (c + 1) * NY]
        back_re, back_im = b[:, :NX], b[:, NX:]
        real += sens_re[c] * back_re + sens_im[c] * back_im
        imag += sens_re[c] * back_im - sens_im[c] * back_re
    both = jnp.concatenate([real, imag], axis=1)
    total = jnp.where(chunk == 0, both, acc_ref[...] + both)
    acc_ref[...] = total
    out_ref[...] = total.astype(BF16).reshape(out_ref.shape)


def pick_kernel(place_ref, sens_ref, out_ref):
    to, frm = iota((64, 128), 0), iota((64, 128), 1)
    turn = as_matrix((to & 15) * Z + (to >> 4) * 2 + (place_ref[0] & 1) == frm)
    for g in range(16 // SHARE):
        for c in range(2):
            picked = matmul(turn, sens_ref[g, 0, c]).astype(BF16)
            out_ref[g * SHARE : (g + 1) * SHARE, c] = picked.reshape(SHARE, 16, 256)


def turn_kernel(place_ref, data_ref, *out_refs):
    to, frm = iota((128, 128), 0), iota((128, 128), 1)
    depth = (((to >> 5) ^ place_ref[2]) << 1) + (((to >> 4) & 1) ^ place_ref[1])
    turn = as_matrix((to & 15) * Z + depth == frm)
    for b in range(data_ref.shape[1]):
        turned = matmul(turn, data_ref[0, b]).astype(BF16).reshape(SHARE, 2, 16, 256)
        for j in range(SHARE):
            out_refs[j][0, :, b * 16 : (b + 1) * 16] = turned[j]


def full(shape):
    return pl.BlockSpec(shape, lambda *_: (0,) * len(shape))


def call(kernel, place, arrays, grid, in_specs, out_specs, out_shape, scratch, name, micros, vmem):
    return pl.pallas_call(
        kernel,
        grid_spec=pltpu.PrefetchScalarGridSpec(
            num_scalar_prefetch=1, grid=grid, in_specs=in_specs, out_specs=out_specs, scratch_shapes=scratch
        ),
        out_shape=out_shape,
        compiler_params=pltpu.CompilerParams(vmem_limit_bytes=vmem * 2**20),
        cost_estimate=pl.CostEstimate(flops=0, bytes_accessed=int(micros * 3e6), transcendentals=0),
        name=name,
    )(place, *arrays)


def weight_slots():
    return pltpu.VMEM((256 // STEP, STEP, 64, 128), BF16), pltpu.SemaphoreType.DMA((256 // STEP,))


def warp_forward(place, columns, weights, prior, current):
    shape = (16, 128 // SHARE, 256)
    return call(
        warp_kernel,
        place,
        (columns, weights, prior, current),
        (256 // STEP,),
        [
            pl.BlockSpec((8 * STEP, 1), lambda i, p: (i, 0)),
            pl.BlockSpec(memory_space=pltpu.HBM),
            full((128, 256)),
            full((128, 256)),
        ],
        full(shape),
        jax.ShapeDtypeStruct(shape, BF16),
        [pltpu.VMEM((128, 256), F32), *weight_slots()],
        "warp_forward",
        8,
        32,
    )


def warp_adjoint(place, columns, rows, weights, parts):
    return call(
        adjoint_kernel,
        place,
        (columns, rows, weights, parts),
        (256 // STEP,),
        [
            pl.BlockSpec((8 * STEP, 1), lambda i, p: (i, 0)),
            pl.BlockSpec((1, 8 * STEP), lambda i, p: (0, i)),
            pl.BlockSpec(memory_space=pltpu.HBM),
            full((16, 128 // SHARE, 256)),
        ],
        [full((128, 256)), full((128, 256))],
        [jax.ShapeDtypeStruct((128, 256), F32), jax.ShapeDtypeStruct((128, 256), BF16)],
        [pltpu.VMEM((128, 256), BF16), pltpu.VMEM((128, 256), F32), *weight_slots()],
        "warp_adjoint",
        8,
        32,
    )


def data_gradient(place, moved, own, other, measured, mask):
    matrix = row_matrix()
    return call(
        data_kernel,
        place,
        (moved, *own, *other, *measured, mask, jnp.asarray(np.concatenate([matrix, matrix.T, column_table()], axis=1))),
        (2, 8 // PAIR),
        [
            pl.BlockSpec((16, 1, 16, 256), lambda z, c, p: (0, z, 0, 0)),
            *[full((16, 2, 16, 256))] * 8,
            *[pl.BlockSpec((2, 1, NY, 256), lambda z, c, p: (0, z, 0, 0))] * 4,
            full((NY, NX)),
            full((256, 1024)),
        ],
        pl.BlockSpec((16, 1, 16, 256), lambda z, c, p: (0, z, 0, 0)),
        jax.ShapeDtypeStruct((16, 2, 16, 256), BF16),
        [pltpu.VMEM((NY, 256), F32)],
        "data_gradient",
        8,
        40,
    )


def pick_share(place, sensitivity):
    return call(
        pick_kernel,
        place,
        (sensitivity.reshape(4, 4, 2, 128, 256),),
        (1,),
        [pl.BlockSpec((4, 1, 2, 128, 256), lambda g, p: (0, p[0] >> 1, 0, 0, 0))],
        full((16, 2, 16, 256)),
        jax.ShapeDtypeStruct((16, 2, 16, 256), BF16),
        [],
        "pick_share",
        1,
        60,
    )


def turn_data(place, data):
    blocks = 16
    return call(
        turn_kernel,
        place,
        (data.reshape(2, 16, 128, 256),),
        (2, 16 // blocks),
        [pl.BlockSpec((1, blocks, 128, 256), lambda c, b, p: (c, b, 0, 0))],
        [pl.BlockSpec((1, 2, 16 * blocks, 256), lambda c, b, p: (c, 0, b, 0))] * SHARE,
        [jax.ShapeDtypeStruct((2, 2, NY, 256), BF16)] * SHARE,
        [],
        "turn_data",
        3,
        60,
    )


def on_device(cine_image, warp_blocks, warp_index, sample_mask, kspace_data, sensitivity):
    loop_axes, coil = ("y", "half", "core"), ("group", "member")
    row, core, member = lax.axis_index("y"), lax.axis_index("core"), lax.axis_index("member")
    offsets = (0, 1, -1, 2)
    place = jnp.stack([row, core, member, *[((row + d) % 4) ^ member for d in offsets]])
    forward = [(i, (i + 1) % 16) for i in range(16)]
    backward = [((i + 1) % 16, i) for i in range(16)]
    current = cine_image.reshape(128, 256)
    prior = lax.ppermute(current, loop_axes, forward)

    sens = pick_share((row * 2 + core).reshape(1), sensitivity)
    prior, kspace_data = lax.optimization_barrier((prior, kspace_data))
    sens = lax.all_to_all(sens, coil, 0, 0, tiled=True)
    measured = turn_data(place, kspace_data)
    measured = [
        piece if j == 0 else lax.ppermute(piece, "member", [(i, i ^ j) for i in range(SHARE)])
        for j, piece in enumerate(measured)
    ]

    weights = warp_blocks.reshape(256, 2, 32, 128).transpose(0, 2, 1, 3).reshape(256, 64, 128)
    weights = pltpu.with_memory_space_constraint(weights, pltpu.HBM)
    index = warp_index[0] - lax.axis_index(coil) * 256
    index = jnp.broadcast_to(index[:, :, None], (256, 2, 4)).reshape(2048)
    columns, rows = index.reshape(2048, 1), index.reshape(1, 2048)
    prior, sens, measured[0], columns = lax.optimization_barrier((prior, sens, measured[0], columns))
    moved = warp_forward(place, columns, weights, prior, current)
    up, down = [(i, (i + 1) % 4) for i in range(4)], [(i, (i - 1) % 4) for i in range(4)]
    shared = [lax.ppermute(sens, "y", down), lax.ppermute(sens, "y", up)]
    shared.append(lax.ppermute(shared[0], "y", down))
    moved = lax.all_to_all(moved, coil, 0, 0, tiled=True).reshape(16, 2, 16, 256)
    sens = [sens, *shared]
    other = [lax.ppermute(piece, "core", [(0, 1), (1, 0)]) for piece in sens]
    moved, sens, other, measured = lax.optimization_barrier((moved, sens, other, measured))
    other = [pltpu.with_memory_space_constraint(piece, pltpu.HBM) for piece in other]
    parts = data_gradient(place, moved, sens, other, measured, sample_mask[0])
    parts = lax.all_to_all(parts, coil, 0, 0, tiled=True).reshape(16, 32, 256)
    grad, pulled = warp_adjoint(place, columns, rows, weights, parts)
    from_next = lax.ppermute(pulled, loop_axes, backward)
    return (grad + from_next.astype(F32)).reshape(1, 16, Z, 256)


def solution(mesh):
    inner = Mesh(mesh.devices.reshape(4, 2, 2, 16 // SHARE, SHARE), ("y", "half", "core", "group", "member"))
    bins, coil = ("y", "half", "core"), ("group", "member")
    return jax.shard_map(
        on_device,
        mesh=inner,
        in_specs=(
            P(bins, coil, None, None),
            P(bins, coil, None, None),
            P(bins, coil, None),
            P(bins, None, None),
            P(bins, coil, None, None, None),
            P(None, coil, None, None),
        ),
        out_specs=P(bins, coil, None, None),
        check_vma=False,
    )
```
